512 devices in a mesh: samp: 64 (over z, x, core), var: 8 (over y).
Axes of the slice: x: 4, y: 8, z: 8, core: 2. Of those that a mesh axis runs over, the one named last changes fastest.
Arguments:
- genotypes: bfloat16 [65536, 12288], P('samp', 'var'), may hold values from 0 to 2, as said below
- start_q: float32 [64, 65536], P(None, 'samp'), may hold values from 0 to 1, as said below
Outputs:
- final_q: float32 [64, 65536], P(None, 'samp')
- final_p: float32 [64, 12288], P(None, 'var')
The draws below stay inside these ranges and needn't reach their ends.
Inputs may be any that keep to these rules, and one draw needn't show every extreme that they name: `genotypes`: genotype counts, whole numbers. `start_q`: nonnegative proportions.
All inputs are finite; a program needn't handle non-finite values.
Results may differ from the reference program's by a relative error of at most 0.001.
Values sent between devices are 32-bit elements; how exact they have to be, the bound alone decides.
A program may use at most 64 MiB of HBM per device.

```python
import jax
import jax.numpy as jnp
from jax import lax

K = 64
VARIANTS = 12288
ITERS = 2
SAMPLES = 65536


def shared_labels(key):
    return jax.random.randint(jax.random.fold_in(key, 7), (SAMPLES,), 0, K)


def draw_genotypes(key, part):
    labels = shared_labels(key)
    pattern = jax.random.randint(jax.random.fold_in(key, 8), (K, VARIANTS), 0, 3)
    noise_part = jax.random.randint(jax.random.fold_in(key, 9), (SAMPLES, VARIANTS), 0, 3)
    keep_mask = jax.random.randint(jax.random.fold_in(key, 10), (SAMPLES, VARIANTS), 0, 2)
    counts = jnp.where(keep_mask == 1, pattern[labels], noise_part)
    return counts.astype(jnp.bfloat16)


def draw_start_q(key, part):
    labels = shared_labels(key)
    onehot = (jnp.arange(K)[:, None] == labels[None, :]).astype(jnp.float32)
    noise_part = jax.random.uniform(jax.random.fold_in(key, 12), (K, SAMPLES), jnp.float32)
    return 0.6 * onehot + 0.4 * noise_part


def setup_inputs(seed: int = 0) -> dict:
    keys = jax.random.split(jax.random.key(seed), 3)
    return {
        "genotypes": draw_genotypes(jax.random.fold_in(keys[2], 71), 0),
        "start_q": draw_start_q(jax.random.fold_in(keys[2], 71), 0),
    }


ridge_term = 1.0

def gram_solve(gram_matrix, right_side):
    eye_matrix = jnp.eye(gram_matrix.shape[0], dtype=jnp.float32)
    factor_low = jnp.linalg.cholesky(gram_matrix + ridge_term * eye_matrix)
    return jax.scipy.linalg.cho_solve((factor_low, True), right_side)

def reference(genotypes, start_q):
    halved = genotypes * jnp.asarray(0.5, dtype=genotypes.dtype)
    ancestry = start_q
    frequency = None
    for iteration in range(ITERS):
        ancestry_b = ancestry.astype(genotypes.dtype)
        cross_p = jnp.dot(ancestry_b.astype(jnp.float32), halved.astype(jnp.float32), preferred_element_type=jnp.float32)
        gram_q = jnp.dot(ancestry, ancestry.T, precision=lax.Precision.HIGHEST)
        frequency = gram_solve(gram_q, cross_p)
        freq_b = frequency.astype(genotypes.dtype)
        cross_q = lax.dot_general(freq_b.astype(jnp.float32), halved.astype(jnp.float32), (((1,), (1,)), ((), ())), preferred_element_type=jnp.float32)
        gram_p = jnp.dot(frequency, frequency.T, precision=lax.Precision.HIGHEST)
        ancestry = gram_solve(gram_p, cross_q)
    return (ancestry, frequency)
```

```python
import jax
import jax.numpy as jnp
from jax import lax
from jax.experimental import pallas as pl
from jax.experimental.pallas import tpu as pltpu
from jax.sharding import Mesh
from jax.sharding import PartitionSpec as P

ITERS = 2
RIDGE = 1.0
K = 64
NZ, NX, NC, NY = 8, 4, 2, 8
S, V = 1024, 1536
SH, VH, VQ = S // 2, V // 2, V // 4
CROSS = 24
TILES = (CROSS + 4, CROSS)
ROWS = (40, 32)
EXACT = lax.Precision.HIGHEST
f32, bf16 = jnp.float32, jnp.bfloat16
MESH = pl.DeviceIdType.MESH


def dot(a, b, precision=None):
    return jnp.dot(a, b, precision=precision, preferred_element_type=f32)


def dot_t(a, b, precision=None):
    return lax.dot_general(
        a, b, (((1,), (1,)), ((), ())), precision=precision, preferred_element_type=f32
    )


def inverse(gram):
    row = lax.broadcasted_iota(jnp.int32, (K, 128), 0)
    lane = lax.broadcasted_iota(jnp.int32, (K, 128), 1)
    m = jnp.where(lane < K, gram + jnp.where(lane == row, RIDGE, 0.0), jnp.where(lane - K == row, 1.0, 0.0))
    sub = lax.broadcasted_iota(jnp.int32, (8, 128), 0)
    for b in range(0, K, 8):
        r = m[b : b + 8, :]
        cs = [jnp.broadcast_to(r[:, b + j : b + j + 1], (8, 128)) for j in range(8)]
        for j in range(8):
            c = cs[j]
            inv = 1.0 / c[j : j + 1, :]
            hit = sub == j
            rn = r[j : j + 1, :] * inv
            r = jnp.where(hit, rn, r - c * rn)
            for i in range(j + 1, 8):
                q = cs[i][j : j + 1, :] * inv
                cs[i] = jnp.where(hit, q, cs[i] - c * q)
        upd = m
        for j in range(8):
            upd = upd - m[:, b + j : b + j + 1] * r[j : j + 1, :]
        parts = ([upd[:b]] if b else []) + [r] + ([upd[b + 8 :]] if b + 8 < K else [])
        m = jnp.concatenate(parts, axis=0)
    return m[:, K:]


def far_first(k, n):
    half = (k + 1) // 2
    return n // 2 + half * (1 - 2 * (k % 2))


def kernel(
    g_ref, q_ref, qo_ref, po_ref,
    x, a, p, acc, qacc, gq, gacc, gbuf,
    cs0, cs1, cr0, cr1, t0, t1, r0, r1, f0, f1, fs0, fs1,
    qs0, qs1, qr0, qr1, qf0, qf1,
    load_sem, out_sem, core_s, core_r, rs_s, rs_r, ag_s, ag_r, cag_s, cag_r, ys_s, ys_r, yg_s, yg_r,
):
    z, xx, c, y = (lax.axis_index(n) for n in ("z", "x", "core", "var"))
    chip = z * NX + xx
    cs, cr, t, r, f, fs = (cs0, cs1), (cr0, cr1), (t0, t1), (r0, r1), (f0, f1), (fs0, fs1)
    qs, qr, qf = (qs0, qs1), (qr0, qr1), (qf0, qf1)
    sibling = {"core": 1 - c}
    lane = lax.broadcasted_iota(jnp.int32, (32, 128), 1)

    j_mine = (xx - z + 2 * NX - 1) % NX
    crossing = j_mine < 3
    even = z % 2 == 0
    owner = (crossing | even, crossing)
    mine = (jnp.where(crossing, 3 * z + j_mine, CROSS + z // 2), 3 * z + j_mine)

    def remote(src, dst, s_sem, r_sem, to):
        return pltpu.make_async_remote_copy(
            src_ref=src, dst_ref=dst, send_sem=s_sem, recv_sem=r_sem, device_id=to, device_id_type=MESH
        )

    def settle(ref, sem):
        pltpu.make_async_copy(ref, ref, sem).wait()

    loads = [
        pltpu.make_async_copy(q_ref, a, load_sem.at[0]),
        pltpu.make_async_copy(g_ref.at[pl.ds(0, SH)], x.at[pl.ds(0, SH)], load_sem.at[1]),
        pltpu.make_async_copy(g_ref.at[pl.ds(SH, SH)], x.at[pl.ds(SH, SH)], load_sem.at[2]),
    ]
    for load in loads:
        load.start()

    barrier = pltpu.get_barrier_semaphore()

    def greet(i, carry):
        to = {"z": (z + i // NX) % NZ, "x": (xx + i % NX) % NX}
        pl.semaphore_signal(barrier, inc=1, device_id=to, device_id_type=MESH)
        return carry

    lax.fori_loop(1, NZ * NX, greet, 0)

    def greet_y(i, carry):
        pl.semaphore_signal(barrier, inc=1, device_id={"var": (y + i) % NY}, device_id_type=MESH)
        return carry

    lax.fori_loop(1, NY, greet_y, 0)
    pl.semaphore_signal(barrier, inc=1, device_id=sibling, device_id_type=MESH)

    def start_columns(h, who):
        return pl.multiple_of(h * VH + VQ * who, 128)

    def samples_part(k, exchange):
        block = a[:, k * SH : (k + 1) * SH]
        half = (block * 0.5).astype(bf16)
        gram = dot_t(block, block, EXACT)
        gq[:, :K] = gram if k == 0 else gq[:, :K] + gram
        for h in range(2):
            for who in (1 - c, c):
                cols = start_columns(h, who)
                part = dot(half, x[k * SH : (k + 1) * SH, pl.ds(cols, VQ)])
                if k:
                    part = part + acc[:, pl.ds(cols, VQ)]
                if not exchange:
                    acc[:, pl.ds(cols, VQ)] = part
                    continue
                out = cs[h] if who is not c else t[h]
                for l in range(3):
                    out[8 * l : 8 * l + 8] = part[:, 128 * l : 128 * l + 128].reshape(8, 8, 128)
                if h == 0:
                    first = pl.multiple_of(32 * who, 32)
                    out[CROSS : CROSS + 4] = gq[pl.ds(first, 32), :].reshape(4, 8, 128)
                if who is not c:
                    remote(cs[h], cr[h], core_s.at[h], core_r.at[h], sibling).start()

    def sum_over_samples(h):
        settle(cr[h], core_r.at[h])
        t[h][...] = t[h][...] + cr[h][...]

        def send(tile, to):
            remote(t[h].at[tile], r[h].at[chip], rs_s.at[h], rs_r.at[h], to).start()

        def cross(i, carry):
            zt = (z + far_first(i // 3, NZ)) % NZ
            j = i % 3
            xt = (zt + 1 + j) % NX

            @pl.when((zt != z) | (xt != xx))
            def _():
                send(3 * zt + j, {"z": zt, "x": xt})

            return carry

        lax.fori_loop(0, CROSS, cross, 0)
        if h == 0:

            def gram(i, carry):
                zt = 2 * i
                xt = zt % NX

                @pl.when((zt != z) | (xt != xx))
                def _():
                    send(CROSS + i, {"z": zt, "x": xt})

                return carry

            lax.fori_loop(0, 4, gram, 0)

    def spread_sums(h):
        @pl.when(owner[h])
        def _():
            settle(r[h].at[pl.ds(0, 31)], rs_r.at[h])
            r[h][chip] = t[h][mine[h]]
            f[h][mine[h]] = jnp.sum(r[h][...], axis=0)

            def send(i, carry):
                zt = (z + far_first(i // NX, NZ)) % NZ
                xt = (xx + far_first(i % NX, NX)) % NX
                tile = f[h].at[mine[h]]
                remote(tile, tile, ag_s.at[h], ag_r.at[h], {"z": zt, "x": xt}).start()
                return carry

            lax.fori_loop(0, NZ * NX - 1, send, 0)

    def to_sibling(h):
        n = TILES[h]

        @pl.when(owner[h])
        def _():
            settle(f[h].at[pl.ds(0, n - 1)], ag_r.at[h])

        @pl.when(jnp.logical_not(owner[h]))
        def _():
            settle(f[h], ag_r.at[h])

        remote(f[h], fs[h], cag_s.at[h], cag_r.at[h], sibling).start()

    def frequencies(h, ginv):
        for src, who in ((f[h], c), (fs[h], 1 - c)):
            if src is fs[h]:
                settle(fs[h], cag_r.at[h])
            total = jnp.concatenate([src[8 * l : 8 * l + 8].reshape(K, 128) for l in range(3)], axis=1)
            p[:, pl.ds(start_columns(h, who), VQ)] = dot(ginv, total, EXACT)

    def send_y(h):
        def send(i, carry):
            yt = (y + far_first(i, NY)) % NY
            remote(qs[h].at[yt], qr[h].at[y], ys_s.at[h], ys_r.at[h], {"var": yt}).start()
            return carry

        lax.fori_loop(0, NY - 1, send, 0)

    def variants_part(h):
        block = p[:, h * VH : (h + 1) * VH]
        half = (block * 0.5).astype(bf16)
        gram = dot_t(block, block, EXACT)
        if h == 0:
            gacc[:, :K] = gram
        else:
            gacc[:, :K] = gacc[:, :K] + gram
            qs[0][:, :8, :] = gacc[...].reshape(8, 8, 128)
        for k in range(2):
            for s in range(k * SH, (k + 1) * SH, 256):
                part = dot_t(half, x[s : s + 256, h * VH : (h + 1) * VH])
                if h == 0:
                    qacc[:, s : s + 256] = part
                    continue
                part = part + qacc[:, s : s + 256]
                for b in range(2):
                    top = part[:32, 128 * b : 128 * b + 128]
                    low = part[32:, 128 * b : 128 * b + 128]
                    peer = (s - k * SH) // 64 + 2 * b
                    at = ROWS[k] - 32
                    qs[k][peer, at:, :] = jnp.where(lane < K, top, pltpu.roll(low, K, 1))
                    qs[k][peer + 1, at:, :] = jnp.where(lane < K, pltpu.roll(top, K, 1), low)
            if h == 1:
                send_y(k)

    def spread_y(k):
        settle(qr[k].at[pl.ds(0, NY - 1)], ys_r.at[k])
        qr[k][y] = qs[k][y]
        qf[k][y] = jnp.sum(qr[k][...], axis=0)

        def send(i, carry):
            yt = (y + far_first(i, NY)) % NY
            mine_y = qf[k].at[y]
            remote(mine_y, mine_y, yg_s.at[k], yg_r.at[k], {"var": yt}).start()
            return carry

        lax.fori_loop(0, NY - 1, send, 0)

    def ancestries(k, hinv):
        at = ROWS[k] - 32
        blocks = []
        for m in range(4):
            one, two = qf[k][2 * m, at:, :], qf[k][2 * m + 1, at:, :]
            top = jnp.where(lane < K, one, pltpu.roll(two, K, 1))
            low = jnp.where(lane < K, pltpu.roll(one, K, 1), two)
            blocks.append(jnp.concatenate([top, low], axis=0))
        a[:, k * SH : (k + 1) * SH] = dot(hinv, jnp.concatenate(blocks, axis=1), EXACT)

    gq[...] = jnp.zeros_like(gq)
    gacc[...] = jnp.zeros_like(gacc)
    loads[0].wait()
    loads[1].wait()
    samples_part(0, False)
    loads[2].wait()
    pl.semaphore_wait(barrier, NZ * NX - 1 + NY - 1 + 1)
    samples_part(1, True)

    def iteration(it, carry):
        sum_over_samples(0)
        sum_over_samples(1)
        spread_sums(0)
        spread_sums(1)
        to_sibling(0)
        settle(fs[0], cag_r.at[0])
        gbuf[pl.ds(4 * c, 4)] = f[0][CROSS:]
        gbuf[pl.ds(4 * (1 - c), 4)] = fs[0][CROSS:]
        ginv = inverse(gbuf[...].reshape(K, 128))
        for src, who in ((f[0], c), (fs[0], 1 - c)):
            total = jnp.concatenate([src[8 * l : 8 * l + 8].reshape(K, 128) for l in range(3)], axis=1)
            p[:, pl.ds(start_columns(0, who), VQ)] = dot(ginv, total, EXACT)
        variants_part(0)
        to_sibling(1)
        frequencies(1, ginv)
        variants_part(1)
        spread_y(0)
        spread_y(1)
        settle(qf[0].at[pl.ds(0, NY - 1)], yg_r.at[0])
        hinv = inverse(qf[0][:, :8, :].reshape(K, 128))
        ancestries(0, hinv)

        for h in range(2):
            settle(cs[h], core_s.at[h])
            settle(fs[h], cag_s.at[h])
            settle(qs[h].at[pl.ds(0, NY - 1)], ys_s.at[h])
            settle(qf[h].at[pl.ds(0, NY - 1)], yg_s.at[h])

            @pl.when(owner[h])
            def _():
                settle(t[h].at[pl.ds(0, TILES[h] - 1)], rs_s.at[h])
                settle(r[h].at[pl.ds(0, 31)], ag_s.at[h])

            @pl.when(jnp.logical_not(owner[h]))
            def _():
                settle(t[h], rs_s.at[h])

        @pl.when(it < ITERS - 1)
        def _():
            samples_part(0, False)

        settle(qf[1].at[pl.ds(0, NY - 1)], yg_r.at[1])
        ancestries(1, hinv)

        @pl.when(it < ITERS - 1)
        def _():
            samples_part(1, True)

        return carry

    lax.fori_loop(0, ITERS, iteration, 0)
    out_p = pltpu.make_async_copy(p, po_ref, out_sem.at[0])
    out_q = pltpu.make_async_copy(a, qo_ref, out_sem.at[1])
    out_p.start()
    out_q.start()
    out_p.wait()
    out_q.wait()


def body(genotypes, start_q):
    def vm(*shape, dtype=f32):
        return pltpu.VMEM(shape, dtype)

    tiles = [vm(n, 8, 128) for n in TILES]
    chips = [vm(NZ * NX, 8, 128)] * 2
    along_y = [vm(NY, n, 128) for n in ROWS]
    sem = pltpu.SemaphoreType.DMA
    return pl.pallas_call(
        kernel,
        out_shape=(
            jax.ShapeDtypeStruct((K, S), f32),
            jax.ShapeDtypeStruct((K, V), f32),
        ),
        in_specs=[pl.BlockSpec(memory_space=pl.ANY)] * 2,
        out_specs=(pl.BlockSpec(memory_space=pl.ANY),) * 2,
        scratch_shapes=[
            vm(S, V, dtype=bf16), vm(K, S), vm(K, V), vm(K, V), vm(K, S), vm(K, 128), vm(K, 128), vm(8, 8, 128),
            *tiles, *tiles, *tiles, *chips, *tiles, *tiles,
            *along_y, *along_y, *along_y,
            sem((3,)), sem((2,)), *[sem((2,))] * 12,
        ],
        compiler_params=pltpu.CompilerParams(
            collective_id=0, has_side_effects=True, vmem_limit_bytes=48 * 2**20
        ),
    )(genotypes, start_q)


def solution(mesh):
    finer = Mesh(mesh.devices.reshape(NZ, NX, NC, NY), ("z", "x", "core", "var"))
    samp = ("z", "x", "core")
    return jax.shard_map(
        body,
        mesh=finer,
        in_specs=(P(samp, "var"), P(None, samp)),
        out_specs=(P(None, samp), P(None, "var")),
        check_vma=False,
    )
```
